32 devices in a mesh: seq: 4 (over z), fsdp: 8 (over y, x, core).
Axes of the slice: x: 2, y: 2, z: 4, core: 2. Of those that a mesh axis runs over, the one named last changes fastest.
Arguments:
- queries: bfloat16 [16, 512, 8192], P('fsdp', None, 'seq'), may hold values from -48 to 48
- d_out: bfloat16 [16, 512, 8192], P('fsdp', None, 'seq'), may hold values from -12 to 12
- keys_values: bfloat16 [16, 512, 2048], P('fsdp', None, 'seq'), may hold values from -4.5 to 4.5
- lengths: int32 [16], P('fsdp'), may hold values from 1 to 512, 2730 in all
- w_kv: bfloat16 [8192, 2048], P('fsdp'), may hold values from -0.125 to 0.125
Outputs:
- d_queries: bfloat16 [16, 512, 8192], P('fsdp', 'seq')
- d_hidden: bfloat16 [16, 512, 8192], P('fsdp', 'seq')
The draws below stay inside these ranges and needn't reach their ends.
All inputs are finite; a program needn't handle non-finite values. No bound on the sum of `lengths` on one device may be relied on, other than what follows from the above.
Results may differ from the reference program's by a relative error of at most 0.009.
Values may be sent and summed in bfloat16 or wider, within the bound.
A program may use at most 192 MiB of HBM per device.

```python
import math
import jax
import jax.numpy as jnp
import numpy as np
from jax import lax

D = 8192
H = 64
KVH = 8
HD = 128
L = 512
R = 16
N_SEQ = 4


def draw_saved(key):
    folded = jax.random.fold_in(key, 4242)
    seed_query, seed_key, seed_value = jax.random.split(folded, 3)
    query_shape = (R, L, H * HD)
    key_shape = (R, L, KVH * HD)
    query_draw = jnp.clip(jax.random.normal(seed_query, query_shape, jnp.float32), -4.5, 4.5)
    key_draw = jnp.clip(jax.random.normal(seed_key, key_shape, jnp.float32), -4.5, 4.5)
    value_draw = jnp.clip(jax.random.normal(seed_value, key_shape, jnp.float32), -4.5, 4.5)
    return (query_draw, jnp.concatenate([key_draw, value_draw], axis=2))


def draw_queries(key, part):
    return draw_saved(key)[0].astype(jnp.bfloat16)


def draw_keys_values(key, part):
    return draw_saved(key)[1].astype(jnp.bfloat16)


def block_levels(stream_key, shape, shards, least, high):
    level, own = 1.0, jax.random.fold_in(stream_key, 6)
    for axis_at, parts in shards:
        draws = jnp.exp(jax.random.uniform(jax.random.fold_in(own, axis_at), (parts,), jnp.float32, least / len(shards), high / len(shards)))
        level = level * jnp.repeat(draws, shape[axis_at] // parts).reshape([-1 if axis == axis_at else 1 for axis in range(len(shape))])
    return level


def length_profile(number_of, total, limit, lean):
    weights = [(1 << 20) // math.isqrt(grade ** lean) + 1 for grade in range(2, number_of + 1)]
    rest, counts = total - limit - (number_of - 1), [1] * (number_of - 1)
    while rest > 0:
        movable = [i for i in range(number_of - 1) if counts[i] < limit]
        mass, budget = sum([weights[i] for i in movable]), rest
        for i in movable:
            extra = min(limit - counts[i], max(1, budget * weights[i] // mass), rest)
            counts[i] = counts[i] + extra
            rest = rest - extra
    return np.array([limit] + counts)


def ragged_sizes(key, number_of, total, most, skew):
    if number_of == 2:
        one = jax.random.randint(key, (), max(1, total - most), min(most, total - 1) + 1)
        return jnp.stack([one, total - one])
    sizes = jnp.asarray(length_profile(number_of, total, most, skew), jnp.int32)
    couples = (number_of - 1) // 2
    donor, taker = sizes[1:1 + 2 * couples:2], sizes[2:2 + 2 * couples:2]
    margin = jnp.minimum(donor - 1, most - taker)
    shifted = jax.random.randint(jax.random.fold_in(key, 1), (couples,), 0, 1 << 20) % (margin + 1)
    sizes = sizes.at[1:1 + 2 * couples:2].set(donor - shifted).at[2:2 + 2 * couples:2].set(taker + shifted)
    return sizes[jax.random.permutation(jax.random.fold_in(key, 2), number_of)]


def scatter_about(own_key, shape, deviation, most, shards=(), kind=jnp.bfloat16):
    entries = deviation * jax.random.normal(own_key, shape, jnp.float32)
    if shards:
        entries = entries * block_levels(own_key, shape, shards, -0.22, 0.18)
    return jnp.clip(entries, -most, most).astype(kind)


def setup_inputs(seed: int = 0) -> dict:
    key_list = jax.random.split(jax.random.key(seed), 6)
    return {
        "queries": draw_queries(jax.random.fold_in(key_list[5], 71), 0),
        "d_out": scatter_about(key_list[1], (R, L, H * HD), 2.0, 12.0, ((0, 8), (2, 4))),
        "keys_values": draw_keys_values(jax.random.fold_in(key_list[5], 71), 0),
        "lengths": ragged_sizes(key_list[3], R, R * L // 3, L, 2).astype(jnp.int32),
        "w_kv": scatter_about(key_list[4], (D, 2 * KVH * HD), (2 * KVH * HD) ** -0.5, 0.125, ((0, 8),)),
    }


def rollout_terms(query_rows, dout_rows, kv_rows, length):
    score_scale = 1.0 / math.sqrt(HD)
    group_size = H // KVH
    shard_rows = L // N_SEQ
    query_split = query_rows.astype(jnp.float32).reshape(L, KVH, group_size, HD)
    grad_split = dout_rows.astype(jnp.float32).reshape(L, KVH, group_size, HD)
    key_split = kv_rows[:, :KVH * HD].astype(jnp.float32).reshape(L, KVH, HD)
    value_split = kv_rows[:, KVH * HD:].astype(jnp.float32).reshape(L, KVH, HD)
    scores = jnp.einsum('icgd,jcd->cgij', query_split, key_split) * score_scale
    positions = jnp.arange(L, dtype=jnp.int32)
    allowed = (positions[None, :] <= positions[:, None]) & (positions[:, None] < length)
    masked = jnp.where(allowed, scores, -1e+30)
    largest = lax.optimization_barrier(jnp.max(masked, axis=-1, keepdims=True))
    numer = jnp.where(allowed, jnp.exp(masked - largest), 0.0)
    totals = lax.optimization_barrier(jnp.sum(numer, axis=-1, keepdims=True))
    probability = numer / jnp.maximum(totals, 1.0)
    prob_half = lax.optimization_barrier(probability.astype(jnp.bfloat16)).astype(jnp.float32)
    output_rec = jnp.einsum('cgij,jcd->icgd', prob_half, value_split)
    row_dot = lax.optimization_barrier(jnp.sum(grad_split * output_rec, axis=-1))
    grad_prob = jnp.einsum('icgd,jcd->cgij', grad_split, value_split)
    grad_score = probability * (grad_prob - jnp.transpose(row_dot, (1, 2, 0))[..., None])
    grad_half = lax.optimization_barrier(grad_score.astype(jnp.bfloat16)).astype(jnp.float32)
    grad_query = (score_scale * jnp.einsum('cgij,jcd->icgd', grad_half, key_split)).astype(jnp.bfloat16)
    grad_query = grad_query.reshape(L, H * HD)
    grad_shards = grad_half.reshape(KVH, group_size, N_SEQ, shard_rows, L)
    prob_shards = prob_half.reshape(KVH, group_size, N_SEQ, shard_rows, L)
    query_shards = query_split.reshape(N_SEQ, shard_rows, KVH, group_size, HD)
    dout_shards = grad_split.reshape(N_SEQ, shard_rows, KVH, group_size, HD)
    grad_key = score_scale * jnp.einsum('cgsij,sicgd->sjcd', grad_shards, query_shards)
    grad_value = jnp.einsum('cgsij,sicgd->sjcd', prob_shards, dout_shards)
    partial_value = jnp.concatenate([grad_key.reshape(N_SEQ, L, KVH * HD), grad_value.reshape(N_SEQ, L, KVH * HD)], axis=-1)
    partial_value = lax.optimization_barrier(partial_value.astype(jnp.bfloat16)).astype(jnp.float32)
    grad_kv = lax.optimization_barrier(jnp.sum(partial_value, axis=0)).astype(jnp.bfloat16)
    return (grad_query, grad_kv)

def reference(queries, d_out, keys_values, lengths, w_kv):
    d_queries, grad_kv = lax.map(lambda members: rollout_terms(*members), (queries, d_out, keys_values, lengths))
    flat = grad_kv.reshape(R * L, 2 * KVH * HD)
    d_hidden = jnp.dot(flat, w_kv.T, preferred_element_type=jnp.float32).astype(jnp.bfloat16)
    return (d_queries, d_hidden.reshape(R, L, D))
```

```python
import functools
import math

import jax
import jax.numpy as jnp
from jax import lax
from jax.experimental import pallas as pl
from jax.experimental.pallas import tpu as pltpu
from jax.sharding import PartitionSpec as P

D = 8192
H = 64
KVH = 8
HD = 128
BLOCK = 128
WIDE = 4


def dot_nt(a, b):
    return lax.dot_general(a, b, (((1,), (1,)), ((), ())), preferred_element_type=jnp.float32)


def dot_nn(a, b):
    return jnp.dot(a, b, preferred_element_type=jnp.float32)


def attention_kernel(r, len_ref, q_ref, g_ref, k_ref, v_ref, dq_ref, dkv_ref, dk_acc, dv_acc):
    rows = q_ref.shape[1]
    group = q_ref.shape[2] // HD
    scale = 1.0 / math.sqrt(HD)
    length = len_ref[r]
    dk_acc[...] = jnp.zeros_like(dk_acc)
    dv_acc[...] = jnp.zeros_like(dv_acc)
    width = WIDE * BLOCK
    for block in range(rows // BLOCK):
        lo, n = block * BLOCK, (block + 1) * BLOCK

        @pl.when(lo >= length)
        def _():
            dq_ref[lo:n, :] = jnp.zeros((BLOCK, group * HD), dq_ref.dtype)

        @pl.when(lo < length)
        def _():
            keys = k_ref[0, :n, :]
            values = v_ref[0, :n, :]
            keys_t = keys.T
            lane = lax.broadcasted_iota(jnp.int32, (1, width), 1) % BLOCK
            live = (lane + lo) < length
            causal = lax.broadcasted_iota(jnp.int32, (BLOCK, width), 0) <= lane
            for first in range(0, group, WIDE):
                heads = range(first, first + WIDE)
                q = jnp.concatenate([q_ref[0, lo:n, h * HD:(h + 1) * HD] for h in heads], axis=0)
                g = jnp.concatenate([g_ref[0, lo:n, h * HD:(h + 1) * HD] for h in heads], axis=0)
                s = dot_nt(keys, q)
                edge = jnp.where(causal, s[lo:], -1e30)
                s = edge if lo == 0 else jnp.concatenate([s[:lo], edge], axis=0)
                m = jnp.max(s, axis=0, keepdims=True)
                e = jnp.exp2((s - m) * (scale * math.log2(math.e)))
                total = jnp.sum(e, axis=0, keepdims=True)
                p = e * jnp.where(live, 1.0 / jnp.maximum(total, 1.0), 0.0)
                half = p.astype(jnp.bfloat16)
                gp = dot_nt(values, g)
                rd = jnp.sum(half.astype(jnp.float32) * gp, axis=0, keepdims=True)
                gs = (p * (gp - rd)).astype(jnp.bfloat16)
                dk_acc[:n, :] += dot_nn(gs, q)
                dv_acc[:n, :] += dot_nn(half, g)
                dq = (dot_nn(keys_t, gs) * scale).astype(jnp.bfloat16)
                for at, h in enumerate(heads):
                    dq_ref[lo:n, h * HD:(h + 1) * HD] = dq[:, at * BLOCK:(at + 1) * BLOCK].T
    dkv_ref[:, :HD] = (dk_acc[...] * scale).astype(jnp.bfloat16)
    dkv_ref[:, HD:] = dv_acc[...].astype(jnp.bfloat16)


def attention(r, lengths, queries, d_out, keys, values):
    _, rows, own_cols = queries.shape
    kv_own = keys.shape[2] // HD
    cols = own_cols // kv_own
    wide = pl.BlockSpec((1, rows, cols), lambda c, _: (r, 0, c))
    thin = pl.BlockSpec((1, rows, HD), lambda c, _: (r, 0, c))
    return pl.pallas_call(
        functools.partial(attention_kernel, r),
        out_shape=(
            jax.ShapeDtypeStruct((rows, own_cols), jnp.bfloat16),
            jax.ShapeDtypeStruct((rows, kv_own * 2 * HD), jnp.bfloat16),
        ),
        grid_spec=pltpu.PrefetchScalarGridSpec(
            num_scalar_prefetch=1,
            grid=(kv_own,),
            in_specs=[wide, wide, thin, thin],
            out_specs=[
                pl.BlockSpec((rows, cols), lambda c, _: (0, c)),
                pl.BlockSpec((rows, 2 * HD), lambda c, _: (0, c)),
            ],
            scratch_shapes=[pltpu.VMEM((rows, HD), jnp.float32)] * 2,
        ),
        compiler_params=pltpu.CompilerParams(vmem_limit_bytes=40 * 2**20),
        cost_estimate=pl.CostEstimate(
            flops=10 * rows * rows * own_cols // 2,
            bytes_accessed=6 * rows * own_cols,
            transcendentals=rows * rows * own_cols // HD // 2,
        ),
    )(lengths, queries, d_out, keys, values)


def local(queries, d_out, keys_values, lengths, w_kv):
    seq = lax.axis_size("seq")
    me = lax.axis_index("seq")
    rollouts, rows, own_cols = queries.shape
    kv_own = KVH // seq
    shard = rows // seq
    w_every = lax.all_gather(w_kv, "fsdp", axis=0, tiled=True)

    half = seq // 2
    chunk = kv_own * HD
    slots = (keys_values[:, :, :chunk], keys_values[:, :, chunk:])
    got = []
    for q in range(2):
        perm = [(t, 2 * t + q) for t in range(half)] + [(half + t, 2 * t + 1 - q) for t in range(half)]
        got.append(lax.ppermute(jnp.where(me < half, slots[q], slots[1 - q]), "seq", perm))
    odd = me % 2 == 1
    keys = jnp.where(odd, got[1], got[0])
    values = jnp.where(odd, got[0], got[1])

    query_parts, kv_parts = [], []
    for r in range(rollouts):
        dq, dkv = attention(r, lengths, queries, d_out, keys, values)
        kv_parts.append(lax.all_to_all(dkv.reshape(seq, shard, 2 * chunk), "seq", 0, 0))
        query_parts.append(lax.all_to_all(dq.reshape(seq, shard, own_cols), "seq", 0, 0))
    d_queries = jnp.stack(query_parts).transpose(0, 2, 1, 3).reshape(rollouts, shard, seq * own_cols)
    kv = jnp.stack(kv_parts).reshape(rollouts, seq, shard, kv_own, 2, HD)
    grad_kv = kv.transpose(0, 2, 4, 1, 3, 5).reshape(rollouts * shard, 2 * KVH * HD)
    d_hidden = lax.dot_general(
        grad_kv, w_every, (((1,), (1,)), ((), ())), preferred_element_type=jnp.float32
    ).astype(jnp.bfloat16)
    return (d_queries, d_hidden.reshape(rollouts, shard, w_every.shape[0]))


def solution(mesh):
    in_specs = (
        P("fsdp", None, "seq"),
        P("fsdp", None, "seq"),
        P("fsdp", None, "seq"),
        P("fsdp"),
        P("fsdp", None),
    )
    out_specs = (P("fsdp", "seq", None), P("fsdp", "seq", None))
    return jax.shard_map(local, mesh=mesh, in_specs=in_specs, out_specs=out_specs, check_vma=False)
```

```python
import functools
import math

import jax
import jax.numpy as jnp
from jax import lax
from jax.experimental import pallas as pl
from jax.experimental.pallas import tpu as pltpu
from jax.sharding import PartitionSpec as P

D = 8192
H = 64
KVH = 8
HD = 128
BLOCK = 128
WIDE = 4


def dot_nt(a, b):
    return lax.dot_general(a, b, (((1,), (1,)), ((), ())), preferred_element_type=jnp.float32)


def dot_nn(a, b):
    return jnp.dot(a, b, preferred_element_type=jnp.float32)


def attention_kernel(len_ref, q_ref, g_ref, k_ref, v_ref, dq_ref, dkv_ref, dk_acc, dv_acc):
    rows = q_ref.shape[1]
    group = q_ref.shape[2] // HD
    scale = 1.0 / math.sqrt(HD)
    length = len_ref[pl.program_id(0)]
    dk_acc[...] = jnp.zeros_like(dk_acc)
    dv_acc[...] = jnp.zeros_like(dv_acc)
    width = WIDE * BLOCK
    for block in range(rows // BLOCK):
        lo, n = block * BLOCK, (block + 1) * BLOCK

        @pl.when(lo >= length)
        def _():
            dq_ref[0, lo:n, :] = jnp.zeros((BLOCK, group * HD), dq_ref.dtype)

        @pl.when(lo < length)
        def _():
            keys = k_ref[0, :n, :]
            values = v_ref[0, :n, :]
            keys_t = keys.T
            lane = lax.broadcasted_iota(jnp.int32, (1, width), 1) % BLOCK
            live = (lane + lo) < length
            causal = lax.broadcasted_iota(jnp.int32, (BLOCK, width), 0) <= lane
            for first in range(0, group, WIDE):
                heads = range(first, first + WIDE)
                q = jnp.concatenate([q_ref[0, lo:n, h * HD:(h + 1) * HD] for h in heads], axis=0)
                g = jnp.concatenate([g_ref[0, lo:n, h * HD:(h + 1) * HD] for h in heads], axis=0)
                s = dot_nt(keys, q)
                edge = jnp.where(causal, s[lo:], -1e30)
                s = edge if lo == 0 else jnp.concatenate([s[:lo], edge], axis=0)
                m = jnp.max(s, axis=0, keepdims=True)
                e = jnp.exp2((s - m) * (scale * math.log2(math.e)))
                total = jnp.sum(e, axis=0, keepdims=True)
                p = e * jnp.where(live, 1.0 / jnp.maximum(total, 1.0), 0.0)
                half = p.astype(jnp.bfloat16)
                gp = dot_nt(values, g)
                rd = jnp.sum(half.astype(jnp.float32) * gp, axis=0, keepdims=True)
                gs = (p * (gp - rd)).astype(jnp.bfloat16)
                dk_acc[:n, :] += dot_nn(gs, q)
                dv_acc[:n, :] += dot_nn(half, g)
                dq = (dot_nn(keys_t, gs) * scale).astype(jnp.bfloat16)
                for at, h in enumerate(heads):
                    dq_ref[0, lo:n, h * HD:(h + 1) * HD] = dq[:, at * BLOCK:(at + 1) * BLOCK].T
    dkv_ref[0, :, :HD] = (dk_acc[...] * scale).astype(jnp.bfloat16)
    dkv_ref[0, :, HD:] = dv_acc[...].astype(jnp.bfloat16)


def attention(lengths, queries, d_out, keys, values):
    rollouts, rows, own_cols = queries.shape
    kv_own = keys.shape[2] // HD
    cols = own_cols // kv_own
    wide = pl.BlockSpec((1, rows, cols), lambda r, c, _: (r, 0, c))
    thin = pl.BlockSpec((1, rows, HD), lambda r, c, _: (r, 0, c))
    return pl.pallas_call(
        attention_kernel,
        out_shape=(
            jax.ShapeDtypeStruct((rollouts, rows, own_cols), jnp.bfloat16),
            jax.ShapeDtypeStruct((rollouts, rows, kv_own * 2 * HD), jnp.bfloat16),
        ),
        grid_spec=pltpu.PrefetchScalarGridSpec(
            num_scalar_prefetch=1,
            grid=(rollouts, kv_own),
            in_specs=[wide, wide, thin, thin],
            out_specs=[
                wide,
                pl.BlockSpec((1, rows, 2 * HD), lambda r, c, _: (r, 0, c)),
            ],
            scratch_shapes=[pltpu.VMEM((rows, HD), jnp.float32)] * 2,
        ),
        compiler_params=pltpu.CompilerParams(vmem_limit_bytes=56 * 2**20),
        cost_estimate=pl.CostEstimate(
            flops=10 * rollouts * rows * rows * own_cols // 2,
            bytes_accessed=6 * rollouts * rows * own_cols,
            transcendentals=rollouts * rows * rows * own_cols // HD // 2,
        ),
    )(lengths, queries, d_out, keys, values)


MESH = pl.DeviceIdType.MESH


def exchange_kernel(
    seq, chips, dq_ref, dkv_ref, w_ref, wx_ref, dqo_ref, dho_ref,
    kv_buf, g_buf, out_buf, kv_send, kv_recv, q_send, q_recv, g_send, g_recv, h_send, h_recv, own_sem,
):
    me, fsdp = lax.axis_index("seq"), lax.axis_index("fsdp")
    chip, core = fsdp // 2, fsdp % 2
    rollouts, rows, own_cols = dq_ref.shape
    shard = rows // seq
    kv_own = KVH // seq
    w_rows = w_ref.shape[0]
    out_cols = 2 * w_rows

    def seq_to(o):
        return lax.rem(me + o, seq)

    def chip_to(o):
        return lax.rem(chip + o, chips)

    def row_part(ref, d):
        return ref.at[:, pl.ds(pl.multiple_of(d * shard, shard), shard), :]

    def columns(ref, at, size):
        return ref.at[:, :, pl.ds(pl.multiple_of(at * size, size), size)]

    barrier = pltpu.get_barrier_semaphore()
    for o in range(1, seq):
        pl.semaphore_signal(barrier, inc=1, device_id={"seq": seq_to(o)}, device_id_type=MESH)
    for o in range(1, chips):
        pl.semaphore_signal(
            barrier, inc=1, device_id={"fsdp": chip_to(o) * 2 + core}, device_id_type=MESH
        )
    pl.semaphore_wait(barrier, seq + chips - 2)

    def seq_copy(o, src, dst, send, recv):
        return pltpu.make_async_remote_copy(
            src_ref=src, dst_ref=dst, send_sem=send.at[o], recv_sem=recv.at[o],
            device_id={"seq": seq_to(o)}, device_id_type=MESH,
        )

    def chip_copy(o, src, dst, send, recv):
        return pltpu.make_async_remote_copy(
            src_ref=src, dst_ref=dst, send_sem=send.at[o], recv_sem=recv.at[o],
            device_id={"fsdp": chip_to(o) * 2 + core}, device_id_type=MESH,
        )

    kv_copies = [
        seq_copy(o, row_part(dkv_ref, seq_to(o)), kv_buf.at[me], kv_send, kv_recv)
        for o in range(1, seq)
    ]
    q_copies = [
        seq_copy(o, row_part(dq_ref, seq_to(o)), columns(dqo_ref, me, own_cols), q_send, q_recv)
        for o in range(1, seq)
    ]
    for copy in kv_copies:
        copy.start()
    kv_local = pltpu.make_async_copy(row_part(dkv_ref, me), kv_buf.at[me], own_sem.at[0])
    kv_local.start()
    q_local = pltpu.make_async_copy(
        row_part(dq_ref, me), columns(dqo_ref, me, own_cols), own_sem.at[1]
    )
    q_local.start()
    kv_local.wait()
    for copy in kv_copies:
        copy.wait()
    for copy in q_copies[::-1]:
        copy.start()

    for src in range(seq):
        for c in range(kv_own):
            for kind in range(2):
                at = kind * KVH * HD + (src * kv_own + c) * HD
                g_buf[chip, :, :, at:at + HD] = kv_buf[src, :, :, (2 * c + kind) * HD:(2 * c + kind + 1) * HD]
    g_copies = [
        chip_copy(o, g_buf.at[chip], g_buf.at[chip], g_send, g_recv) for o in range(1, chips)
    ]
    for copy in g_copies:
        copy.start()

    tile = min(512, w_rows)

    def project(src):
        x = g_buf[src].reshape(rollouts * shard, 2 * KVH * HD)
        for half, w in enumerate((w_ref, wx_ref)):
            start = (core if half == 0 else 1 - core) * w_rows

            @pl.loop(0, w_rows // tile)
            def _(t):
                y = dot_nt(x, w[pl.ds(pl.multiple_of(t * tile, tile), tile), :])
                y = y.astype(jnp.bfloat16).reshape(rollouts, shard, tile)
                out_buf[src, :, :, pl.ds(pl.multiple_of(start + t * tile, tile), tile)] = y

    project(chip)
    h_local = pltpu.make_async_copy(
        out_buf.at[chip], columns(dho_ref, chip, out_cols), own_sem.at[2]
    )
    h_local.start()
    h_copies = []
    for o in range(1, chips):
        g_copies[o - 1].wait_recv()
        src = chip_to(chips - o)
        project(src)
        copy = chip_copy(
            chips - o, out_buf.at[src], columns(dho_ref, chip, out_cols), h_send, h_recv
        )
        copy.start()
        h_copies.append(copy)
    for copy in g_copies:
        copy.wait_send()
    q_local.wait()
    h_local.wait()
    for copy in q_copies:
        copy.wait()
    for copy in h_copies:
        copy.wait()


def exchange(dq, dkv, w, w_other):
    seq = lax.axis_size("seq")
    chips = lax.axis_size("fsdp") // 2
    rollouts, rows, own_cols = dq.shape
    shard = rows // seq
    vmem = pl.BlockSpec(memory_space=pltpu.VMEM)
    hbm = pl.BlockSpec(memory_space=pl.ANY)
    dma = pltpu.SemaphoreType.DMA
    return pl.pallas_call(
        functools.partial(exchange_kernel, seq, chips),
        out_shape=(
            jax.ShapeDtypeStruct((rollouts, shard, seq * own_cols), jnp.bfloat16),
            jax.ShapeDtypeStruct((rollouts, shard, 2 * chips * w.shape[0]), jnp.bfloat16),
        ),
        in_specs=[hbm, hbm, vmem, vmem],
        out_specs=[hbm, hbm],
        scratch_shapes=[
            pltpu.VMEM((seq, rollouts, shard, dkv.shape[2]), jnp.bfloat16),
            pltpu.VMEM((chips, rollouts, shard, 2 * KVH * HD), jnp.bfloat16),
            pltpu.VMEM((chips, rollouts, shard, 2 * w.shape[0]), jnp.bfloat16),
            dma((seq,)), dma((seq,)), dma((seq,)), dma((seq,)),
            dma((chips,)), dma((chips,)), dma((chips,)), dma((chips,)), dma((3,)),
        ],
        compiler_params=pltpu.CompilerParams(
            collective_id=0, has_side_effects=True, vmem_limit_bytes=48 * 2**20
        ),
    )(dq, dkv, w, w_other)


def local(queries, d_out, keys_values, lengths, w_kv):
    seq = lax.axis_size("seq")
    me = lax.axis_index("seq")
    kv_own = KVH // seq
    pairs = [(i, i ^ 1) for i in range(lax.axis_size("fsdp"))]

    half = seq // 2
    chunk = kv_own * HD
    slots = (keys_values[:, :, :chunk], keys_values[:, :, chunk:])
    got = []
    for q in range(2):
        perm = [(t, 2 * t + q) for t in range(half)] + [(half + t, 2 * t + 1 - q) for t in range(half)]
        got.append(lax.ppermute(jnp.where(me < half, slots[q], slots[1 - q]), "seq", perm))
    w_other = lax.ppermute(w_kv, "fsdp", pairs)
    odd = me % 2 == 1
    keys = jnp.where(odd, got[1], got[0])
    values = jnp.where(odd, got[0], got[1])
    dq, dkv = attention(lengths, queries, d_out, keys, values)
    return exchange(dq, dkv, w_kv, w_other)


def solution(mesh):
    in_specs = (
        P("fsdp", None, "seq"),
        P("fsdp", None, "seq"),
        P("fsdp", None, "seq"),
        P("fsdp"),
        P("fsdp", None),
    )
    out_specs = (P("fsdp", "seq", None), P("fsdp", "seq", None))
    return jax.shard_map(local, mesh=mesh, in_specs=in_specs, out_specs=out_specs, check_vma=False)
```

```python
import functools
import math

import jax
import jax.numpy as jnp
from jax import lax
from jax.experimental import pallas as pl
from jax.experimental.pallas import tpu as pltpu
from jax.sharding import PartitionSpec as P

D = 8192
H = 64
KVH = 8
HD = 128
BLOCK = 128
WIDE = 4


def dot_nt(a, b):
    return lax.dot_general(a, b, (((1,), (1,)), ((), ())), preferred_element_type=jnp.float32)


def dot_nn(a, b):
    return jnp.dot(a, b, preferred_element_type=jnp.float32)


def attention_kernel(len_ref, q_ref, g_ref, k_ref, v_ref, dq_ref, dkv_ref, dk_acc, dv_acc):
    rows = q_ref.shape[1]
    group = q_ref.shape[2] // HD
    scale = 1.0 / math.sqrt(HD)
    length = len_ref[pl.program_id(0)]
    dk_acc[...] = jnp.zeros_like(dk_acc)
    dv_acc[...] = jnp.zeros_like(dv_acc)
    width = WIDE * BLOCK
    for block in range(rows // BLOCK):
        lo, n = block * BLOCK, (block + 1) * BLOCK

        @pl.when(lo >= length)
        def _():
            dq_ref[0, lo:n, :] = jnp.zeros((BLOCK, group * HD), dq_ref.dtype)

        @pl.when(lo < length)
        def _():
            keys = k_ref[0, :n, :]
            values = v_ref[0, :n, :]
            keys_t = keys.T
            lane = lax.broadcasted_iota(jnp.int32, (1, width), 1) % BLOCK
            live = (lane + lo) < length
            causal = lax.broadcasted_iota(jnp.int32, (BLOCK, width), 0) <= lane
            for first in range(0, group, WIDE):
                heads = range(first, first + WIDE)
                q = jnp.concatenate([q_ref[0, lo:n, h * HD:(h + 1) * HD] for h in heads], axis=0)
                g = jnp.concatenate([g_ref[0, lo:n, h * HD:(h + 1) * HD] for h in heads], axis=0)
                s = dot_nt(keys, q)
                edge = jnp.where(causal, s[lo:], -1e30)
                s = edge if lo == 0 else jnp.concatenate([s[:lo], edge], axis=0)
                m = jnp.max(s, axis=0, keepdims=True)
                e = jnp.exp2((s - m) * (scale * math.log2(math.e)))
                total = jnp.sum(e, axis=0, keepdims=True)
                p = e * jnp.where(live, 1.0 / jnp.maximum(total, 1.0), 0.0)
                half = p.astype(jnp.bfloat16)
                gp = dot_nt(values, g)
                rd = jnp.sum(half.astype(jnp.float32) * gp, axis=0, keepdims=True)
                gs = (p * (gp - rd)).astype(jnp.bfloat16)
                dk_acc[:n, :] += dot_nn(gs, q)
                dv_acc[:n, :] += dot_nn(half, g)
                dq = (dot_nn(keys_t, gs) * scale).astype(jnp.bfloat16)
                for at, h in enumerate(heads):
                    dq_ref[0, lo:n, h * HD:(h + 1) * HD] = dq[:, at * BLOCK:(at + 1) * BLOCK].T
    dkv_ref[0, :, :HD] = (dk_acc[...] * scale).astype(jnp.bfloat16)
    dkv_ref[0, :, HD:] = dv_acc[...].astype(jnp.bfloat16)


def attention(lengths, queries, d_out, keys, values):
    rollouts, rows, own_cols = queries.shape
    kv_own = keys.shape[2] // HD
    cols = own_cols // kv_own
    wide = pl.BlockSpec((1, rows, cols), lambda r, c, _: (r, 0, c))
    thin = pl.BlockSpec((1, rows, HD), lambda r, c, _: (r, 0, c))
    return pl.pallas_call(
        attention_kernel,
        out_shape=(
            jax.ShapeDtypeStruct((rollouts, rows, own_cols), jnp.bfloat16),
            jax.ShapeDtypeStruct((rollouts, rows, kv_own * 2 * HD), jnp.bfloat16),
        ),
        grid_spec=pltpu.PrefetchScalarGridSpec(
            num_scalar_prefetch=1,
            grid=(rollouts, kv_own),
            in_specs=[wide, wide, thin, thin],
            out_specs=[
                wide,
                pl.BlockSpec((1, rows, 2 * HD), lambda r, c, _: (r, 0, c)),
            ],
            scratch_shapes=[pltpu.VMEM((rows, HD), jnp.float32)] * 2,
        ),
        compiler_params=pltpu.CompilerParams(vmem_limit_bytes=56 * 2**20),
        cost_estimate=pl.CostEstimate(
            flops=10 * rollouts * rows * rows * own_cols // 2,
            bytes_accessed=6 * rollouts * rows * own_cols,
            transcendentals=rollouts * rows * rows * own_cols // HD // 2,
        ),
    )(lengths, queries, d_out, keys, values)


MESH = pl.DeviceIdType.MESH


def exchange_kernel(
    seq, chips, dq_ref, dkv_ref, w_ref, wx_ref, dqo_ref, dho_ref,
    kv_buf, g_buf, out_buf, kv_send, kv_recv, q_send, q_recv, g_send, g_recv, h_send, h_recv, own_sem,
):
    me, fsdp = lax.axis_index("seq"), lax.axis_index("fsdp")
    chip, core = fsdp // 2, fsdp % 2
    rollouts, rows, own_cols = dq_ref.shape
    shard = rows // seq
    kv_own = KVH // seq
    w_rows = w_ref.shape[0]
    out_cols = 2 * w_rows

    def seq_to(o):
        return lax.rem(me + o, seq)

    def chip_to(o):
        return lax.rem(chip + o, chips)

    def row_part(ref, d):
        return ref.at[:, pl.ds(pl.multiple_of(d * shard, shard), shard), :]

    def columns(ref, at, size):
        return ref.at[:, :, pl.ds(pl.multiple_of(at * size, size), size)]

    barrier = pltpu.get_barrier_semaphore()
    for o in range(1, seq):
        pl.semaphore_signal(barrier, inc=1, device_id={"seq": seq_to(o)}, device_id_type=MESH)
    for o in range(1, chips):
        pl.semaphore_signal(
            barrier, inc=1, device_id={"fsdp": chip_to(o) * 2 + core}, device_id_type=MESH
        )
    pl.semaphore_wait(barrier, seq + chips - 2)

    def seq_copy(o, src, dst, send, recv):
        return pltpu.make_async_remote_copy(
            src_ref=src, dst_ref=dst, send_sem=send.at[o], recv_sem=recv.at[o],
            device_id={"seq": seq_to(o)}, device_id_type=MESH,
        )

    def chip_copy(o, src, dst, send, recv):
        return pltpu.make_async_remote_copy(
            src_ref=src, dst_ref=dst, send_sem=send.at[o], recv_sem=recv.at[o],
            device_id={"fsdp": chip_to(o) * 2 + core}, device_id_type=MESH,
        )

    kv_copies = [
        seq_copy(o, row_part(dkv_ref, seq_to(o)), kv_buf.at[me], kv_send, kv_recv)
        for o in range(1, seq)
    ]
    q_copies = [
        seq_copy(o, row_part(dq_ref, seq_to(o)), columns(dqo_ref, me, own_cols), q_send, q_recv)
        for o in range(1, seq)
    ]
    for copy in kv_copies:
        copy.start()
    kv_local = pltpu.make_async_copy(row_part(dkv_ref, me), kv_buf.at[me], own_sem.at[0])
    kv_local.start()
    q_local = pltpu.make_async_copy(
        row_part(dq_ref, me), columns(dqo_ref, me, own_cols), own_sem.at[1]
    )
    q_local.start()
    kv_local.wait()
    for copy in kv_copies:
        copy.wait()
    for copy in q_copies:
        copy.start()

    for src in range(seq):
        for c in range(kv_own):
            for kind in range(2):
                at = kind * KVH * HD + (src * kv_own + c) * HD
                g_buf[chip, :, :, at:at + HD] = kv_buf[src, :, :, (2 * c + kind) * HD:(2 * c + kind + 1) * HD]
    g_copies = [
        chip_copy(o, g_buf.at[chip], g_buf.at[chip], g_send, g_recv) for o in range(1, chips)
    ]
    for copy in g_copies:
        copy.start()

    tile = min(512, w_rows)

    def project(src):
        x = g_buf[src].reshape(rollouts * shard, 2 * KVH * HD)
        for half, w in enumerate((w_ref, wx_ref)):
            start = (core if half == 0 else 1 - core) * w_rows

            @pl.loop(0, w_rows // tile)
            def _(t):
                y = dot_nt(x, w[pl.ds(pl.multiple_of(t * tile, tile), tile), :])
                y = y.astype(jnp.bfloat16).reshape(rollouts, shard, tile)
                out_buf[src, :, :, pl.ds(pl.multiple_of(start + t * tile, tile), tile)] = y

    project(chip)
    h_local = pltpu.make_async_copy(
        out_buf.at[chip], columns(dho_ref, chip, out_cols), own_sem.at[2]
    )
    h_local.start()
    h_copies = []
    for o in range(1, chips):
        g_copies[o - 1].wait_recv()
        src = chip_to(chips - o)
        project(src)
        copy = chip_copy(
            chips - o, out_buf.at[src], columns(dho_ref, chip, out_cols), h_send, h_recv
        )
        copy.start()
        h_copies.append(copy)
    for copy in g_copies:
        copy.wait_send()
    q_local.wait()
    h_local.wait()
    for copy in q_copies:
        copy.wait()
    for copy in h_copies:
        copy.wait()


def exchange(dq, dkv, w, w_other):
    seq = lax.axis_size("seq")
    chips = lax.axis_size("fsdp") // 2
    rollouts, rows, own_cols = dq.shape
    shard = rows // seq
    vmem = pl.BlockSpec(memory_space=pltpu.VMEM)
    hbm = pl.BlockSpec(memory_space=pl.ANY)
    dma = pltpu.SemaphoreType.DMA
    return pl.pallas_call(
        functools.partial(exchange_kernel, seq, chips),
        out_shape=(
            jax.ShapeDtypeStruct((rollouts, shard, seq * own_cols), jnp.bfloat16),
            jax.ShapeDtypeStruct((rollouts, shard, 2 * chips * w.shape[0]), jnp.bfloat16),
        ),
        in_specs=[hbm, hbm, vmem, vmem],
        out_specs=[hbm, hbm],
        scratch_shapes=[
            pltpu.VMEM((seq, rollouts, shard, dkv.shape[2]), jnp.bfloat16),
            pltpu.VMEM((chips, rollouts, shard, 2 * KVH * HD), jnp.bfloat16),
            pltpu.VMEM((chips, rollouts, shard, 2 * w.shape[0]), jnp.bfloat16),
            dma((seq,)), dma((seq,)), dma((seq,)), dma((seq,)),
            dma((chips,)), dma((chips,)), dma((chips,)), dma((chips,)), dma((3,)),
        ],
        compiler_params=pltpu.CompilerParams(
            collective_id=0, has_side_effects=True, vmem_limit_bytes=48 * 2**20
        ),
    )(dq, dkv, w, w_other)


def local(queries, d_out, keys_values, lengths, w_kv):
    seq = lax.axis_size("seq")
    me = lax.axis_index("seq")
    kv_own = KVH // seq
    pairs = [(i, i ^ 1) for i in range(lax.axis_size("fsdp"))]

    half = seq // 2
    chunk = kv_own * HD
    slots = (keys_values[:, :, :chunk], keys_values[:, :, chunk:])
    got = []
    for q in range(2):
        perm = [(t, 2 * t + q) for t in range(half)] + [(half + t, 2 * t + 1 - q) for t in range(half)]
        got.append(lax.ppermute(jnp.where(me < half, slots[q], slots[1 - q]), "seq", perm))
    w_other = lax.ppermute(w_kv, "fsdp", pairs)
    odd = me % 2 == 1
    keys = jnp.where(odd, got[1], got[0])
    values = jnp.where(odd, got[0], got[1])
    dq, dkv = attention(lengths, queries, d_out, keys, values)
    return exchange(dq, dkv, w_kv, w_other)


def solution(mesh):
    in_specs = (
        P("fsdp", None, "seq"),
        P("fsdp", None, "seq"),
        P("fsdp", None, "seq"),
        P("fsdp"),
        P("fsdp", None),
    )
    out_specs = (P("fsdp", "seq", None), P("fsdp", "seq", None))
    return jax.shard_map(local, mesh=mesh, in_specs=in_specs, out_specs=out_specs, check_vma=False)
```

```python
import functools
import math

import jax
import jax.numpy as jnp
from jax import lax
from jax.experimental import pallas as pl
from jax.experimental.pallas import tpu as pltpu
from jax.sharding import PartitionSpec as P

D = 8192
H = 64
KVH = 8
HD = 128
BLOCK = 128
WIDE = 4


def dot_nt(a, b):
    return lax.dot_general(a, b, (((1,), (1,)), ((), ())), preferred_element_type=jnp.float32)


def dot_nn(a, b):
    return jnp.dot(a, b, preferred_element_type=jnp.float32)


def attention_kernel(len_ref, q_ref, g_ref, k_ref, v_ref, dq_ref, dkv_ref, dk_acc, dv_acc):
    rows = q_ref.shape[1]
    group = q_ref.shape[2] // HD
    scale = 1.0 / math.sqrt(HD)
    length = len_ref[pl.program_id(0)]
    dk_acc[...] = jnp.zeros_like(dk_acc)
    dv_acc[...] = jnp.zeros_like(dv_acc)
    width = WIDE * BLOCK
    for block in range(rows // BLOCK):
        lo, n = block * BLOCK, (block + 1) * BLOCK

        @pl.when(lo >= length)
        def _():
            dq_ref[0, lo:n, :] = jnp.zeros((BLOCK, group * HD), dq_ref.dtype)

        @pl.when(lo < length)
        def _():
            keys = k_ref[0, :n, :]
            values = v_ref[0, :n, :]
            keys_t = keys.T
            lane = lax.broadcasted_iota(jnp.int32, (1, width), 1) % BLOCK
            live = (lane + lo) < length
            causal = lax.broadcasted_iota(jnp.int32, (BLOCK, width), 0) <= lane
            for first in range(0, group, WIDE):
                heads = range(first, first + WIDE)
                q = jnp.concatenate([q_ref[0, lo:n, h * HD:(h + 1) * HD] for h in heads], axis=0)
                g = jnp.concatenate([g_ref[0, lo:n, h * HD:(h + 1) * HD] for h in heads], axis=0)
                s = dot_nt(keys, q)
                edge = jnp.where(causal, s[lo:], -1e30)
                s = edge if lo == 0 else jnp.concatenate([s[:lo], edge], axis=0)
                m = jnp.max(s, axis=0, keepdims=True)
                e = jnp.exp2((s - m) * (scale * math.log2(math.e)))
                total = jnp.sum(e, axis=0, keepdims=True)
                p = e * jnp.where(live, 1.0 / jnp.maximum(total, 1.0), 0.0)
                half = p.astype(jnp.bfloat16)
                gp = dot_nt(values, g)
                rd = jnp.sum(half.astype(jnp.float32) * gp, axis=0, keepdims=True)
                gs = (p * (gp - rd)).astype(jnp.bfloat16)
                dk_acc[:n, :] += dot_nn(gs, q)
                dv_acc[:n, :] += dot_nn(half, g)
                dq = (dot_nn(keys_t, gs) * scale).astype(jnp.bfloat16)
                for at, h in enumerate(heads):
                    dq_ref[0, lo:n, h * HD:(h + 1) * HD] = dq[:, at * BLOCK:(at + 1) * BLOCK].T
    dkv_ref[0, :, :HD] = (dk_acc[...] * scale).astype(jnp.bfloat16)
    dkv_ref[0, :, HD:] = dv_acc[...].astype(jnp.bfloat16)


def attention(lengths, queries, d_out, keys, values):
    rollouts, rows, own_cols = queries.shape
    kv_own = keys.shape[2] // HD
    cols = own_cols // kv_own
    wide = pl.BlockSpec((1, rows, cols), lambda r, c, _: (r, 0, c))
    thin = pl.BlockSpec((1, rows, HD), lambda r, c, _: (r, 0, c))
    return pl.pallas_call(
        attention_kernel,
        out_shape=(
            jax.ShapeDtypeStruct((rollouts, rows, own_cols), jnp.bfloat16),
            jax.ShapeDtypeStruct((rollouts, rows, kv_own * 2 * HD), jnp.bfloat16),
        ),
        grid_spec=pltpu.PrefetchScalarGridSpec(
            num_scalar_prefetch=1,
            grid=(rollouts, kv_own),
            in_specs=[wide, wide, thin, thin],
            out_specs=[
                wide,
                pl.BlockSpec((1, rows, 2 * HD), lambda r, c, _: (r, 0, c)),
            ],
            scratch_shapes=[pltpu.VMEM((rows, HD), jnp.float32)] * 2,
        ),
        compiler_params=pltpu.CompilerParams(vmem_limit_bytes=56 * 2**20),
        cost_estimate=pl.CostEstimate(
            flops=10 * rollouts * rows * rows * own_cols // 2,
            bytes_accessed=6 * rollouts * rows * own_cols,
            transcendentals=rollouts * rows * rows * own_cols // HD // 2,
        ),
    )(lengths, queries, d_out, keys, values)


MESH = pl.DeviceIdType.MESH


def exchange_kernel(
    seq, chips, dq_ref, dkv_ref, w_ref, wx_ref, dqo_ref, dho_ref,
    kv_buf, g_buf, out_buf, kv_send, kv_recv, q_send, q_recv, g_send, g_recv, h_send, h_recv, own_sem,
):
    me, fsdp = lax.axis_index("seq"), lax.axis_index("fsdp")
    chip, core = fsdp // 2, fsdp % 2
    rollouts, rows, own_cols = dq_ref.shape
    shard = rows // seq
    kv_own = KVH // seq
    w_rows = w_ref.shape[0]
    out_cols = 2 * w_rows

    def seq_to(o):
        return lax.rem(me + o, seq)

    def chip_to(o):
        return lax.rem(chip + o, chips)

    def row_part(ref, d):
        return ref.at[:, pl.ds(pl.multiple_of(d * shard, shard), shard), :]

    def columns(ref, at, size):
        return ref.at[:, :, pl.ds(pl.multiple_of(at * size, size), size)]

    barrier = pltpu.get_barrier_semaphore()
    for o in range(1, seq):
        pl.semaphore_signal(barrier, inc=1, device_id={"seq": seq_to(o)}, device_id_type=MESH)
    for o in range(1, chips):
        pl.semaphore_signal(
            barrier, inc=1, device_id={"fsdp": chip_to(o) * 2 + core}, device_id_type=MESH
        )
    pl.semaphore_wait(barrier, seq + chips - 2)

    def seq_copy(o, src, dst, send, recv):
        return pltpu.make_async_remote_copy(
            src_ref=src, dst_ref=dst, send_sem=send.at[o], recv_sem=recv.at[o],
            device_id={"seq": seq_to(o)}, device_id_type=MESH,
        )

    def chip_copy(o, src, dst, send, recv):
        return pltpu.make_async_remote_copy(
            src_ref=src, dst_ref=dst, send_sem=send.at[o], recv_sem=recv.at[o],
            device_id={"fsdp": chip_to(o) * 2 + core}, device_id_type=MESH,
        )

    kv_copies = [
        seq_copy(o, row_part(dkv_ref, seq_to(o)), kv_buf.at[me], kv_send, kv_recv)
        for o in range(1, seq)
    ]
    q_copies = [
        seq_copy(o, row_part(dq_ref, seq_to(o)), columns(dqo_ref, me, own_cols), q_send, q_recv)
        for o in range(1, seq)
    ]
    for copy in kv_copies:
        copy.start()
    kv_local = pltpu.make_async_copy(row_part(dkv_ref, me), kv_buf.at[me], own_sem.at[0])
    kv_local.start()
    q_local = pltpu.make_async_copy(
        row_part(dq_ref, me), columns(dqo_ref, me, own_cols), own_sem.at[1]
    )
    q_local.start()
    kv_local.wait()
    for copy in kv_copies:
        copy.wait()
    for copy in q_copies:
        copy.start()

    for src in range(seq):
        for c in range(kv_own):
            for kind in range(2):
                at = kind * KVH * HD + (src * kv_own + c) * HD
                g_buf[chip, :, :, at:at + HD] = kv_buf[src, :, :, (2 * c + kind) * HD:(2 * c + kind + 1) * HD]
    g_copies = [
        chip_copy(o, g_buf.at[chip], g_buf.at[chip], g_send, g_recv) for o in range(1, chips)
    ]
    for copy in g_copies:
        copy.start()

    tile = min(512, w_rows)

    def project(src, send):
        x = g_buf[src].reshape(rollouts * shard, 2 * KVH * HD)
        for half, w in enumerate((w_ref, wx_ref)):
            start = (core if half == 0 else 1 - core) * w_rows

            @pl.loop(0, w_rows // tile)
            def _(t):
                y = dot_nt(x, w[pl.ds(pl.multiple_of(t * tile, tile), tile), :])
                y = y.astype(jnp.bfloat16).reshape(rollouts, shard, tile)
                out_buf[src, :, :, pl.ds(pl.multiple_of(start + t * tile, tile), tile)] = y

            send(half)

    project(chip, lambda part: None)
    h_local = pltpu.make_async_copy(
        out_buf.at[chip], columns(dho_ref, chip, out_cols), own_sem.at[2]
    )
    h_local.start()
    h_copies = []
    for o in range(1, chips):
        g_copies[o - 1].wait_recv()
        back = chips - o
        src = chip_to(back)

        def send(half, src=src, back=back):
            part = core if half == 0 else 1 - core
            copy = chip_copy(
                back, columns(out_buf.at[src], part, w_rows), columns(dho_ref, 2 * chip + part, w_rows),
                h_send.at[half], h_recv.at[half],
            )
            copy.start()
            h_copies.append(copy)

        project(src, send)
    for copy in g_copies:
        copy.wait_send()
    q_local.wait()
    h_local.wait()
    for copy in q_copies:
        copy.wait()
    for copy in h_copies:
        copy.wait()


def exchange(dq, dkv, w, w_other):
    seq = lax.axis_size("seq")
    chips = lax.axis_size("fsdp") // 2
    rollouts, rows, own_cols = dq.shape
    shard = rows // seq
    vmem = pl.BlockSpec(memory_space=pltpu.VMEM)
    hbm = pl.BlockSpec(memory_space=pl.ANY)
    dma = pltpu.SemaphoreType.DMA
    return pl.pallas_call(
        functools.partial(exchange_kernel, seq, chips),
        out_shape=(
            jax.ShapeDtypeStruct((rollouts, shard, seq * own_cols), jnp.bfloat16),
            jax.ShapeDtypeStruct((rollouts, shard, 2 * chips * w.shape[0]), jnp.bfloat16),
        ),
        in_specs=[hbm, hbm, vmem, vmem],
        out_specs=[hbm, hbm],
        scratch_shapes=[
            pltpu.VMEM((seq, rollouts, shard, dkv.shape[2]), jnp.bfloat16),
            pltpu.VMEM((chips, rollouts, shard, 2 * KVH * HD), jnp.bfloat16),
            pltpu.VMEM((chips, rollouts, shard, 2 * w.shape[0]), jnp.bfloat16),
            dma((seq,)), dma((seq,)), dma((seq,)), dma((seq,)),
            dma((chips,)), dma((chips,)), dma((2, chips)), dma((2, chips)), dma((3,)),
        ],
        compiler_params=pltpu.CompilerParams(
            collective_id=0, has_side_effects=True, vmem_limit_bytes=48 * 2**20
        ),
    )(dq, dkv, w, w_other)


def local(queries, d_out, keys_values, lengths, w_kv):
    seq = lax.axis_size("seq")
    me = lax.axis_index("seq")
    kv_own = KVH // seq
    pairs = [(i, i ^ 1) for i in range(lax.axis_size("fsdp"))]

    half = seq // 2
    chunk = kv_own * HD
    slots = (keys_values[:, :, :chunk], keys_values[:, :, chunk:])
    got = []
    for q in range(2):
        perm = [(t, 2 * t + q) for t in range(half)] + [(half + t, 2 * t + 1 - q) for t in range(half)]
        got.append(lax.ppermute(jnp.where(me < half, slots[q], slots[1 - q]), "seq", perm))
    w_other = lax.ppermute(w_kv, "fsdp", pairs)
    odd = me % 2 == 1
    keys = jnp.where(odd, got[1], got[0])
    values = jnp.where(odd, got[0], got[1])
    dq, dkv = attention(lengths, queries, d_out, keys, values)
    return exchange(dq, dkv, w_kv, w_other)


def solution(mesh):
    in_specs = (
        P("fsdp", None, "seq"),
        P("fsdp", None, "seq"),
        P("fsdp", None, "seq"),
        P("fsdp"),
        P("fsdp", None),
    )
    out_specs = (P("fsdp", "seq", None), P("fsdp", "seq", None))
    return jax.shard_map(local, mesh=mesh, in_specs=in_specs, out_specs=out_specs, check_vma=False)
```
